32 devices in a mesh: section: 4 (over y, x), shard: 8 (over z, core).
Axes of the slice: x: 2, y: 2, z: 4, core: 2. Of those that a mesh axis runs over, the one named last changes fastest.
Arguments:
- memory: bfloat16 [8192, 512], P('shard'), may hold values from -6 to 6
- messages: bfloat16 [2, 8, 8, 4, 512], P(None, 'shard', None, 'section'), may hold values from -6 to 6
- slot_rows: int32 [2, 8, 8, 4], P(None, 'shard', None, 'section'), may hold values from 0 to 1023, as said below
- counts: int32 [2, 8, 8], P(None, 'shard'), may hold values from 0 to 4, as said below
- src_slot: int32 [2, 4096], P(None, ('section', 'shard')), may hold values from 0 to 7
- nbr_slots: int32 [2, 4096, 10], P(None, ('section', 'shard')), may hold values from 0 to 7
- time_gap: float32 [2, 4096, 10], P(None, ('section', 'shard')), may hold values from 0.1 to 100
- time_freq: float32 [128], replicated, may hold values from 0.01 to 1
- time_phase: float32 [128], replicated, may hold values from -3.140625 to 3.140625
- gru_input: bfloat16 [512, 1536], P('section'), may hold values from -0.25 to 0.25
- gru_hidden: bfloat16 [512, 1536], P('section'), may hold values from -0.25 to 0.25
- gru_bias: float32 [2, 1536], replicated, may hold values from -3 to 3
- attn_qkv: bfloat16 [512, 1536], P('section'), may hold values from -0.25 to 0.25
- attn_out: bfloat16 [512, 512], P('section'), may hold values from -0.25 to 0.25
- time_proj: bfloat16 [128, 1024], P('section'), may hold values from -0.5 to 0.5
Outputs:
- memory_out: bfloat16 [8192, 512], P('shard')
- embeddings: bfloat16 [2, 4096, 512], P(None, ('section', 'shard'))
The draws below stay inside these ranges and needn't reach their ends.
Inputs may be any that keep to these rules, and one draw needn't show every extreme that they name: `slot_rows`: within one batch the rows of one owner named by all devices' slots are distinct. `counts`: in every batch one owner receives 4 live slots from every device.
All inputs are finite; a program needn't handle non-finite values.
Results may differ from the reference program's by a relative error of at most 0.015.
Values may be sent and summed in bfloat16 or wider, within the bound.
A program may use at most 128 MiB of HBM per device.

```python
import math
import jax
import jax.numpy as jnp
from jax import lax

F = 512
TE = 128
HEADS = 2
HD = 256
NBR = 10
CAP = 4
BATCHES = 2
NODES_DEV = 1024
EV_DEV = 128
NODES = 8192
EVENTS = 4096
POOL = 8
N_SECTION = 4
N_SHARD = 8


def draw_slot_rows(key, part):
    key = jax.random.fold_in(key, 11)
    marks = jax.random.randint(key, (BATCHES, N_SHARD, NODES_DEV), 0, 2 ** 16)
    scores = marks * NODES_DEV + jnp.arange(NODES_DEV, dtype=jnp.int32)[None, None, :]
    order = jnp.argsort(scores, axis=-1, stable=True).astype(jnp.int32)
    taken = order[:, :, :N_SHARD * CAP].reshape(BATCHES, N_SHARD, N_SHARD, CAP)
    return jnp.transpose(taken, (0, 2, 1, 3)).astype(jnp.int32)


def draw_counts(key, part):
    key = jax.random.fold_in(key, 23)
    first, second, third = jax.random.split(key, 3)
    ceiling = jax.random.randint(first, (BATCHES, 1, N_SHARD), 1, 2 * CAP + 1)
    raw = jax.random.randint(second, (BATCHES, N_SHARD, N_SHARD), 0, 2 ** 16) % ceiling
    loads = jnp.minimum(raw, CAP)
    busy = jax.random.randint(third, (BATCHES, 1, 1), 0, N_SHARD)
    full = jnp.arange(N_SHARD, dtype=jnp.int32)[None, None, :] == busy
    return jnp.where(full, CAP, loads).astype(jnp.int32)


def set_ends(drawn, own_key, least, high):
    longest = drawn.shape.index(max(drawn.shape))
    spots = []
    for shift in (0, 1):
        where = [jax.random.randint(jax.random.fold_in(own_key, axis), (), 0, length) for axis, length in enumerate(drawn.shape)]
        where[longest] = (where[longest] + shift) % drawn.shape[longest]
        spots.append(tuple(where))
    return drawn.at[spots[0]].set(least).at[spots[1]].set(high)


def level_of(rng, extent, cuts, smallest, largest):
    def one(position, shards_of):
        draws = jax.random.uniform(jax.random.fold_in(jax.random.fold_in(rng, 6), position), (shards_of,), jnp.float32, smallest / len(cuts), largest / len(cuts))
        return jnp.repeat(jnp.exp(draws), extent[position] // shards_of).reshape((-1,) + (1,) * (len(extent) - position - 1))

    factor_of = one(*cuts[0])
    for cut in cuts[1:]:
        factor_of = factor_of * one(*cut)
    return factor_of


def normal_values(key, dims, deviation, limit, cuts=(), kind=jnp.bfloat16):
    level = level_of(key, dims, cuts, -0.22, 0.18) if cuts else 1.0
    drawn = jax.random.normal(key, dims, jnp.float32) * deviation * level
    return jnp.minimum(jnp.maximum(drawn, -limit), limit).astype(kind)


def setup_inputs(seed: int = 0) -> dict:
    streams_of = jax.random.split(jax.random.key(seed), 16)
    return {
        "memory": normal_values(streams_of[0], (NODES, F), 1.0, 6.0, ((0, 8),)),
        "messages": normal_values(streams_of[1], (BATCHES, N_SHARD, N_SHARD, CAP, F), 1.0, 6.0, ((1, 8), (3, 4))),
        "slot_rows": draw_slot_rows(jax.random.fold_in(streams_of[15], 71), 0),
        "counts": draw_counts(jax.random.fold_in(streams_of[15], 71), 0),
        "src_slot": set_ends(jax.random.randint(streams_of[4], (BATCHES, EVENTS), 0, POOL), jax.random.fold_in(streams_of[4], 1), 0, POOL - 1).astype(jnp.int32),
        "nbr_slots": set_ends(jax.random.randint(streams_of[5], (BATCHES, EVENTS, NBR), 0, POOL), jax.random.fold_in(streams_of[5], 1), 0, POOL - 1).astype(jnp.int32),
        "time_gap": jnp.clip(jnp.exp(math.log(100.0) - 6.9077553 * jax.random.uniform(streams_of[6], (BATCHES, EVENTS, NBR), jnp.float32) ** level_of(streams_of[6], (BATCHES, EVENTS, NBR), ((1, 32),), -0.2, 0.2)), 0.1, 100.0),
        "time_freq": jnp.clip(jnp.exp(jax.random.uniform(streams_of[7], (TE,), jnp.float32, math.log(0.01), math.log(1.0))), 0.01, 1.0),
        "time_phase": jnp.clip(jax.random.uniform(streams_of[8], (TE,), jnp.float32, -3.140625, 3.140625), -3.140625, 3.140625),
        "gru_input": normal_values(streams_of[9], (F, 3 * F), F ** -0.5, 0.25, ((0, 4),)),
        "gru_hidden": normal_values(streams_of[10], (F, 3 * F), F ** -0.5, 0.25, ((0, 4),)),
        "gru_bias": normal_values(streams_of[11], (2, 3 * F), 0.5, 3.0, (), jnp.float32),
        "attn_qkv": normal_values(streams_of[12], (F, 3 * F), F ** -0.5, 0.25, ((0, 4),)),
        "attn_out": normal_values(streams_of[13], (F, F), F ** -0.5, 0.25, ((0, 4),)),
        "time_proj": normal_values(streams_of[14], (TE, 2 * F), TE ** -0.5, 0.5, ((0, 4),)),
    }


def gru_rows(x, h, w_in, w_hid, bias):
    width = x.shape[1]
    gx = jnp.dot(x, w_in, preferred_element_type=jnp.float32) + bias[0]
    gh = jnp.dot(h, w_hid, preferred_element_type=jnp.float32) + bias[1]
    reset = jax.nn.sigmoid(gx[:, :width] + gh[:, :width])
    update = jax.nn.sigmoid(gx[:, width:2 * width] + gh[:, width:2 * width])
    fresh = jnp.tanh(gx[:, 2 * width:] + reset * gh[:, 2 * width:])
    return ((1.0 - update) * fresh + update * h.astype(jnp.float32)).astype(jnp.bfloat16)

def embed(pool, source, nearby, gaps, freq, phase, qkv, out_w, tproj):
    width = pool.shape[1]
    events = source.shape[0]
    kv = jnp.dot(pool, qkv[:, width:], preferred_element_type=jnp.float32).astype(jnp.bfloat16)
    query = jnp.dot(pool[source], qkv[:, :width], preferred_element_type=jnp.float32)
    encoded = jnp.cos(gaps[..., None] * freq + phase).astype(jnp.bfloat16)
    timed = jnp.einsum('ent,tc->enc', encoded.astype(jnp.float32), tproj.astype(jnp.float32))
    near = kv[nearby].astype(jnp.float32) + timed
    keys = near[..., :width].reshape(events, NBR, HEADS, HD)
    values = near[..., width:].reshape(events, NBR, HEADS, HD)
    scores = jnp.einsum('ehd,enhd->ehn', query.reshape(events, HEADS, HD), keys) / jnp.sqrt(jnp.float32(HD))
    weights = jax.nn.softmax(scores, axis=-1)
    mixed = jnp.einsum('ehn,enhd->ehd', weights, values).reshape(events, width).astype(jnp.bfloat16)
    return jnp.dot(mixed, out_w, preferred_element_type=jnp.float32).astype(jnp.bfloat16)

def reference(memory, messages, slot_rows, counts, src_slot, nbr_slots, time_gap, time_freq, time_phase, gru_input, gru_hidden, gru_bias, attn_qkv, attn_out, time_proj):
    quarter = CAP // N_SECTION
    devices = N_SECTION * N_SHARD
    owners = jnp.arange(N_SHARD, dtype=jnp.int32)
    slots = jnp.arange(CAP, dtype=jnp.int32)
    outputs = []
    for batch in range(BATCHES):
        live = slots[None, None, :] < counts[batch][:, :, None]
        node = owners[None, :, None] * NODES_DEV + slot_rows[batch]
        fetched = jnp.where(live[..., None], memory[node], jnp.zeros((), jnp.bfloat16))

        def one_source(pair):
            return gru_rows(pair[0], pair[1], gru_input, gru_hidden, gru_bias)
        updated = lax.map(one_source, (messages[batch].reshape(N_SHARD, N_SHARD * CAP, F), fetched.reshape(N_SHARD, N_SHARD * CAP, F)))
        updated = updated.reshape(N_SHARD, N_SHARD, CAP, F)
        target = jnp.where(live, node, NODES).reshape(-1)
        memory = memory.at[target].set(updated.reshape(-1, F), mode='drop')
        pools = updated.reshape(N_SHARD, N_SHARD, N_SECTION, quarter, F).transpose(2, 0, 1, 3, 4).reshape(devices, POOL, F)

        def one_device(items):
            return embed(items[0], items[1], items[2], items[3], time_freq, time_phase, attn_qkv, attn_out, time_proj)
        result = lax.map(one_device, (pools, src_slot[batch].reshape(devices, EV_DEV), nbr_slots[batch].reshape(devices, EV_DEV, NBR), time_gap[batch].reshape(devices, EV_DEV, NBR)))
        outputs.append(result.reshape(EVENTS, F))
    return (memory, jnp.stack(outputs))
```

```python
import functools

import jax
import jax.numpy as jnp
from jax import lax
from jax.experimental import pallas as pl
from jax.experimental.pallas import tpu as pltpu
from jax.sharding import PartitionSpec as P

HEADS = 2
HD = 256
BATCHES = 2
MESH = pl.DeviceIdType.MESH
F32 = jnp.float32
BF16 = jnp.bfloat16
COS = (
    1.0,
    -0.5,
    0.0416666641831398,
    -0.0013888862449675798,
    2.480053444742225e-05,
    -2.753448029579886e-07,
    2.060102088918825e-09,
    -9.714491364110067e-12,
)


def cosine(x):
    turns = jnp.round(x * 0.15915494309189535)
    r = x - turns * 6.28125
    r = r - turns * 0.001935307179586232
    u = r * r
    total = jnp.full_like(u, COS[-1])
    for c in COS[-2::-1]:
        total = total * u + c
    return total


def dot(a, b, contract=(1, 0), precision=None):
    return lax.dot_general(
        a,
        b,
        (((contract[0],), (contract[1],)), ((), ())),
        preferred_element_type=F32,
        precision=precision,
    )


def split(x):
    high = x.astype(BF16)
    return high, (x - high.astype(F32)).astype(BF16)


def kernel(
    n_sec,
    n_shard,
    memory,
    messages,
    marks,
    src,
    nbr,
    gap,
    freq,
    phase,
    w_in,
    w_hid,
    bias,
    w_qkv,
    w_out,
    w_time,
    memory_out,
    emb,
    all_marks,
    x_src,
    x_all,
    picks_src0,
    picks_src1,
    picks0,
    picks1,
    part_src0,
    part_src1,
    part0,
    part1,
    back_src0,
    back_src1,
    back0,
    back1,
    hot0,
    hot1,
    gates_x,
    te,
    f_qkv,
    f_out,
    f_time,
    send_sems,
    recv_sems,
    bulk_send,
    bulk_recv,
    fwd_send,
    fwd_recv,
    own_sems,
):
    sec = lax.axis_index("section")
    shard = lax.axis_index("shard")
    devices = n_sec * n_shard
    me = sec * n_shard + shard
    nodes, width = memory.shape
    pool = n_shard
    cols = width // n_sec
    events = emb.shape[1]
    nbrs = gap.shape[1]
    tw = freq.shape[0]
    core = lax.rem(shard, 2)
    sibling = shard + 1 - 2 * core
    picks_src, picks = (picks_src0, picks_src1), (picks0, picks1)
    part_src, part = (part_src0, part_src1), (part0, part1)
    back_src, back = (back_src0, back_src1), (back0, back1)
    hot = (hot0, hot1)

    def drain(ref, sem):
        pltpu.make_async_copy(ref, ref, sem).wait()

    def to_all(step):
        def go(j, carry):
            peer = lax.rem(me + j, devices)
            step(lax.div(peer, n_shard), lax.rem(peer, n_shard))
            return carry

        lax.fori_loop(1, devices, go, 0)

    barrier = pltpu.get_barrier_semaphore()
    to_all(
        lambda s, d: pl.semaphore_signal(barrier, inc=1, device_id=(s, d), device_id_type=MESH)
    )

    for s in range(n_sec):
        x_src[s] = messages[:, s * cols : (s + 1) * cols].astype(F32)
    x_all[sec] = x_src[sec]
    all_marks[me] = marks[...]
    weights = ((w_qkv, f_qkv), (w_out, f_out), (w_time, f_time))
    own = []
    for i, (w, full) in enumerate(weights):
        k = w.shape[0]
        copy = pltpu.make_async_copy(
            w, full.at[pl.ds(pl.multiple_of(sec * k, k), k)], own_sems.at[i]
        )
        copy.start()
        own.append(copy)

    pl.semaphore_wait(barrier, devices - 1)

    def send_marks(s, d):
        pltpu.make_async_remote_copy(
            marks, all_marks.at[me], send_sems.at[0], recv_sems.at[0], (s, d), MESH
        ).start()

    to_all(send_marks)
    for j in range(1, n_sec):
        s = lax.rem(sec + j, n_sec)
        pltpu.make_async_remote_copy(
            x_src.at[s], x_all.at[sec], send_sems.at[1], recv_sems.at[1], (s, shard), MESH
        ).start()
    for i, (w, full) in enumerate(weights):
        k = w.shape[0]
        half = k // 2
        here = pl.multiple_of(core * half, half)
        there = pl.multiple_of(sec * k + core * half, half)
        for j in range(1, n_sec):
            s = lax.rem(sec + j, n_sec)
            pltpu.make_async_remote_copy(
                w.at[pl.ds(here, half)],
                full.at[pl.ds(there, half)],
                bulk_send.at[i],
                bulk_recv.at[i],
                (s, shard),
                MESH,
            ).start()

    def time_codes(b):
        for n in range(nbrs):
            x = freq[...] * gap[b, n : n + 1, :] + phase[...]
            te[b, :, n * events : (n + 1) * events] = cosine(x).astype(BF16)

    time_codes(0)

    drain(all_marks.at[pl.ds(0, devices - 1)], recv_sems.at[0])
    lane = lax.broadcasted_iota(jnp.int32, (devices, 128), 1)
    node = lax.broadcasted_iota(jnp.int32, (devices, nodes), 1)
    for b in range(BATCHES):
        row = jnp.sum(jnp.where(lane == shard, all_marks[:, b, :], 0), axis=1, keepdims=True)
        hot[b][...] = jnp.where(row == node, 1.0, 0.0).astype(BF16)
    columns = pl.ds(pl.multiple_of(sec * cols, cols), cols)
    mine = memory[:, columns]

    def send_picks(b, rows):
        for s in range(n_sec):
            block = rows[s * n_shard : (s + 1) * n_shard]
            picks_src[b][:, s, :] = block
        picks[b][shard] = picks_src[b][shard]

        def go(j, carry):
            d = lax.rem(shard + j, n_shard)
            pltpu.make_async_remote_copy(
                picks_src[b].at[d],
                picks[b].at[shard],
                send_sems.at[2 + b],
                recv_sems.at[2 + b],
                (sec, d),
                MESH,
            ).start()
            return carry

        lax.fori_loop(1, n_shard, go, 0)

    send_picks(0, dot(hot0[...], mine))
    before = dot(hot1[...], mine)
    match = dot(hot1[...], hot0[...], (1, 1))
    fresh_rows = jnp.sum(match, axis=1, keepdims=True)
    match = match.astype(BF16)

    drain(x_all.at[pl.ds(0, n_sec - 1)], recv_sems.at[1])
    for b in range(BATCHES):
        rows = jnp.concatenate(
            [x_all[s, b * pool : (b + 1) * pool, :] for s in range(n_sec)], axis=0
        )
        gates_x[b] = dot(rows.astype(BF16), w_in[...])
    time_codes(1)

    def send_parts(b):
        drain(picks[b].at[pl.ds(0, n_shard - 1)], recv_sems.at[2 + b])
        h = jnp.concatenate([picks[b][:, s, :] for s in range(n_sec)], axis=0)
        gh = dot(h.astype(BF16), w_hid[...])
        gx = gates_x[b]
        low = gx[:, : 2 * width] + gh[:, : 2 * width]
        every = jnp.concatenate([low, gx[:, 2 * width :], gh[:, 2 * width :], h, h], axis=1)
        half = every.shape[1] // 2
        for s in range(n_sec):
            block = every[s * pool : (s + 1) * pool]
            part_src[b][s] = jnp.concatenate([block[:, :half], block[:, half:]], axis=0).astype(BF16)
        part[b][sec] = part_src[b][sec]
        for j in range(1, n_sec):
            s = lax.rem(sec + j, n_sec)
            pltpu.make_async_remote_copy(
                part_src[b].at[s],
                part[b].at[sec],
                send_sems.at[4 + b],
                recv_sems.at[4 + b],
                (s, shard),
                MESH,
            ).start()

    def gru(b):
        drain(part[b].at[pl.ds(0, n_sec - 1)], recv_sems.at[4 + b])
        pieces = [part[b][s].astype(F32) for s in range(n_sec)]
        total = functools.reduce(lambda a, c: a + c, pieces)
        gates = jnp.concatenate([total[:pool], total[pool:]], axis=1)
        h = jnp.concatenate([p[pool:, -cols:] for p in pieces], axis=1)
        both = bias[0:1, :] + bias[1:2, :]
        r = jax.nn.sigmoid(gates[:, :width] + both[:, :width])
        z = jax.nn.sigmoid(gates[:, width : 2 * width] + both[:, width : 2 * width])
        gx_n = gates[:, 2 * width : 3 * width] + bias[0:1, 2 * width :]
        gh_n = gates[:, 3 * width : 4 * width] + bias[1:2, 2 * width :]
        n = jnp.tanh(gx_n + r * gh_n)
        updated = ((1.0 - z) * n + z * h).astype(BF16)
        wide = updated.astype(F32)
        for k in range(n_sec):
            back_src[b][:, k, :] = wide[:, k * cols : (k + 1) * cols]
        back[b][me] = back_src[b][shard]

        def send(s, d):
            pltpu.make_async_remote_copy(
                back_src[b].at[d],
                back[b].at[me],
                send_sems.at[6 + b],
                recv_sems.at[6 + b],
                (s, d),
                MESH,
            ).start()

        to_all(send)
        return updated

    def forward():
        for copy in own:
            copy.wait()
        for i, (w, full) in enumerate(weights):
            k = w.shape[0]
            half = k // 2
            drain(full.at[pl.ds(0, (n_sec - 1) * half)], bulk_recv.at[i])
            for j in range(1, n_sec):
                s = lax.rem(sec + j, n_sec)
                place = full.at[pl.ds(pl.multiple_of(s * k + core * half, half), half)]
                pltpu.make_async_remote_copy(
                    place, place, fwd_send.at[i], fwd_recv.at[i], (sec, sibling), MESH
                ).start()

    def gathered():
        for i, (w, full) in enumerate(weights):
            drain(full.at[pl.ds(0, (n_sec - 1) * (w.shape[0] // 2))], fwd_recv.at[i])

    def attend(b, updated):
        qkv = dot(updated, f_qkv[...])
        query = qkv[:, :width]
        keys = qkv[:, width : 2 * width].astype(BF16)
        values = qkv[:, 2 * width :].astype(BF16)
        slot = lax.broadcasted_iota(jnp.int32, (pool, events), 0)
        source = (slot == src[b : b + 1, :]).astype(F32)
        near = [(slot == nbr[b, n : n + 1, :]).astype(F32) for n in range(nbrs)]
        codes = [te[b, :, n * events : (n + 1) * events] for n in range(nbrs)]
        scale = HD ** -0.5
        mixed = []
        for head in range(HEADS):
            low = head * HD
            q_high, q_low = split(query[:, low : low + HD] * scale)
            key = keys[:, low : low + HD]
            proj = f_time[:, low : low + HD]
            pairs = dot(key, q_high, (1, 1)) + dot(key, q_low, (1, 1))
            p_high, p_low = split(pairs)
            hot_source = source.astype(BF16)
            table = dot(p_high, hot_source) + dot(p_low, hot_source)
            turned = dot(q_high, proj, (1, 1)) + dot(q_low, proj, (1, 1))
            t_high, t_low = split(turned)
            scores = []
            for n in range(nbrs):
                timed = dot(t_high, codes[n]) + dot(t_low, codes[n])
                scores.append(
                    jnp.sum(timed * source + table * near[n], axis=0, keepdims=True)
                )
            top = functools.reduce(jnp.maximum, scores)
            powers = [jnp.exp(x - top) for x in scores]
            inverse = 1.0 / functools.reduce(lambda a, c: a + c, powers)
            shares = [x * inverse for x in powers]
            by_code = shares[0] * codes[0].astype(F32)
            by_slot = shares[0] * near[0]
            for n in range(1, nbrs):
                by_code = by_code + shares[n] * codes[n].astype(F32)
                by_slot = by_slot + shares[n] * near[n]
            low_v = width + low
            mixed.append(
                dot(by_code.astype(BF16), f_time[:, low_v : low_v + HD], (0, 0))
                + dot(by_slot.astype(BF16), values[:, low : low + HD], (0, 0))
            )
        joined = jnp.concatenate(mixed, axis=1).astype(BF16)
        emb[b] = dot(joined, f_out[...]).astype(BF16)

    def returned(b, k):
        return back[b][:, k, :].astype(BF16)

    send_parts(0)
    updated0 = gru(0)
    forward()

    drain(back0.at[pl.ds(0, devices - 1)], recv_sems.at[6])
    changed = returned(0, 0)
    for k in range(1, n_sec):
        changed = jnp.where(sec == k, returned(0, k), changed)
    send_picks(1, jnp.where(fresh_rows > 0.5, dot(match, changed), before))

    def write(b, old):
        ones = jnp.ones((devices, cols), BF16)
        tile = 256
        for t in range(0, nodes, tile):
            places = hot[b][:, t : t + tile]
            hit = dot(places, ones, (0, 0)) > 0.5
            for k in range(n_sec):
                spot = slice(k * cols, (k + 1) * cols)
                new = dot(places, returned(b, k), (0, 0))
                kept = old[t : t + tile, spot].astype(F32)
                memory_out[t : t + tile, spot] = jnp.where(hit, new, kept).astype(BF16)

    write(0, memory)
    send_parts(1)
    gathered()
    attend(0, updated0)
    updated1 = gru(1)
    attend(1, updated1)
    drain(back1.at[pl.ds(0, devices - 1)], recv_sems.at[7])
    write(1, memory_out)

    drain(all_marks.at[pl.ds(0, devices - 1)], send_sems.at[0])
    drain(x_all.at[pl.ds(0, n_sec - 1)], send_sems.at[1])
    for b in range(BATCHES):
        drain(picks[b].at[pl.ds(0, n_shard - 1)], send_sems.at[2 + b])
        drain(part[b].at[pl.ds(0, n_sec - 1)], send_sems.at[4 + b])
        drain(back[b].at[pl.ds(0, devices - 1)], send_sems.at[6 + b])
    for i, (w, full) in enumerate(weights):
        rows = pl.ds(0, (n_sec - 1) * (w.shape[0] // 2))
        drain(full.at[rows], bulk_send.at[i])
        drain(full.at[rows], fwd_send.at[i])


def body(
    n_sec,
    n_shard,
    memory,
    messages,
    slot_rows,
    counts,
    src_slot,
    nbr_slots,
    time_gap,
    time_freq,
    time_phase,
    gru_input,
    gru_hidden,
    gru_bias,
    attn_qkv,
    attn_out,
    time_proj,
):
    width = memory.shape[1]
    nodes = memory.shape[0]
    pool = n_shard
    cols = width // n_sec
    events = src_slot.shape[1]
    nbrs = nbr_slots.shape[2]
    tw = time_freq.shape[0]
    devices = n_sec * n_shard
    sec = lax.axis_index("section")
    marks = jnp.where(sec < counts[:, 0, :], slot_rows[:, 0, :, 0], -1)
    marks = jnp.pad(marks, ((0, 8 - BATCHES), (0, 128 - n_shard)))
    wide = (4 * width + 2 * cols) // 2
    out = pl.pallas_call(
        functools.partial(kernel, n_sec, n_shard),
        out_shape=(
            jax.ShapeDtypeStruct((nodes, width), BF16),
            jax.ShapeDtypeStruct((BATCHES, events, width), BF16),
        ),
        in_specs=[pl.BlockSpec(memory_space=pltpu.VMEM)] * 14,
        out_specs=(pl.BlockSpec(memory_space=pltpu.VMEM),) * 2,
        scratch_shapes=[
            pltpu.VMEM((devices, 8, 128), jnp.int32),
            pltpu.VMEM((n_sec, BATCHES * pool, cols), F32),
            pltpu.VMEM((n_sec, BATCHES * pool, cols), F32),
            pltpu.VMEM((n_shard, 8, cols), F32),
            pltpu.VMEM((n_shard, 8, cols), F32),
            pltpu.VMEM((n_shard, 8, cols), F32),
            pltpu.VMEM((n_shard, 8, cols), F32),
            pltpu.VMEM((n_sec, 2 * pool, wide), BF16),
            pltpu.VMEM((n_sec, 2 * pool, wide), BF16),
            pltpu.VMEM((n_sec, 2 * pool, wide), BF16),
            pltpu.VMEM((n_sec, 2 * pool, wide), BF16),
            pltpu.VMEM((n_shard, 8, cols), F32),
            pltpu.VMEM((n_shard, 8, cols), F32),
            pltpu.VMEM((devices, 8, cols), F32),
            pltpu.VMEM((devices, 8, cols), F32),
            pltpu.VMEM((devices, nodes), BF16),
            pltpu.VMEM((devices, nodes), BF16),
            pltpu.VMEM((BATCHES, n_sec * pool, 3 * width), F32),
            pltpu.VMEM((BATCHES, tw, nbrs * events), BF16),
            pltpu.VMEM((width, 3 * width), BF16),
            pltpu.VMEM((width, width), BF16),
            pltpu.VMEM((tw, 2 * width), BF16),
            pltpu.SemaphoreType.DMA((8,)),
            pltpu.SemaphoreType.DMA((8,)),
            pltpu.SemaphoreType.DMA((3,)),
            pltpu.SemaphoreType.DMA((3,)),
            pltpu.SemaphoreType.DMA((3,)),
            pltpu.SemaphoreType.DMA((3,)),
            pltpu.SemaphoreType.DMA((3,)),
        ],
        compiler_params=pltpu.CompilerParams(
            collective_id=0, has_side_effects=True, vmem_limit_bytes=56 * 1024 * 1024
        ),
    )(
        memory,
        messages.reshape(BATCHES * pool, width),
        marks,
        src_slot,
        nbr_slots.transpose(0, 2, 1),
        time_gap.transpose(0, 2, 1),
        time_freq.reshape(tw, 1),
        time_phase.reshape(tw, 1),
        gru_input,
        gru_hidden,
        gru_bias,
        attn_qkv,
        attn_out,
        time_proj,
    )
    return out


def solution(mesh):
    in_specs = (
        P("shard", None),
        P(None, "shard", None, "section", None),
        P(None, "shard", None, "section"),
        P(None, "shard", None),
        P(None, ("section", "shard")),
        P(None, ("section", "shard"), None),
        P(None, ("section", "shard"), None),
        P(),
        P(),
        P("section", None),
        P("section", None),
        P(),
        P("section", None),
        P("section", None),
        P("section", None),
    )
    out_specs = (P("shard", None), P(None, ("section", "shard"), None))
    program = functools.partial(body, mesh.shape["section"], mesh.shape["shard"])
    return jax.shard_map(program, mesh=mesh, in_specs=in_specs, out_specs=out_specs, check_vma=False)
```

```python
import functools

import jax
import jax.numpy as jnp
from jax import lax
from jax.experimental import pallas as pl
from jax.experimental.pallas import tpu as pltpu
from jax.sharding import PartitionSpec as P

HEADS = 2
HD = 256
BATCHES = 2
MESH = pl.DeviceIdType.MESH
F32 = jnp.float32
BF16 = jnp.bfloat16
COS = (
    1.0,
    -0.5,
    0.0416666641831398,
    -0.0013888862449675798,
    2.480053444742225e-05,
    -2.753448029579886e-07,
    2.060102088918825e-09,
    -9.714491364110067e-12,
)


def cosine(x):
    turns = jnp.round(x * 0.15915494309189535)
    r = x - turns * 6.28125
    r = r - turns * 0.001935307179586232
    u = r * r
    total = jnp.full_like(u, COS[-1])
    for c in COS[-2::-1]:
        total = total * u + c
    return total


def wrap(i, n):
    return jnp.where(i >= n, i - n, i)


def dot(a, b, contract=(1, 0), precision=None):
    return lax.dot_general(
        a,
        b,
        (((contract[0],), (contract[1],)), ((), ())),
        preferred_element_type=F32,
        precision=precision,
    )


def split(x):
    high = x.astype(BF16)
    return high, (x - high.astype(F32)).astype(BF16)


def kernel(
    n_sec,
    n_shard,
    memory_hbm,
    messages,
    slot_rows,
    counts,
    src,
    nbr,
    gap,
    freq,
    phase,
    w_in_hbm,
    w_hid_hbm,
    bias,
    w_qkv,
    w_out,
    w_time,
    memory_out,
    emb,
    all_marks,
    x_src,
    x_all,
    picks_src0,
    picks_src1,
    picks0,
    picks1,
    part_src0,
    part_src1,
    part0,
    part1,
    back_src0,
    back_src1,
    back0,
    back1,
    hot0,
    hot1,
    gates_x,
    te,
    f_qkv,
    f_out,
    f_time,
    send_sems,
    recv_sems,
    bulk_send,
    bulk_recv,
    fwd_send,
    fwd_recv,
    own_sems,
    memory,
    w_in,
    w_hid,
    load_sems,
    marks,
):
    sec = lax.axis_index("section")
    shard = lax.axis_index("shard")
    devices = n_sec * n_shard
    me = sec * n_shard + shard
    nodes, width = memory.shape
    pool = n_shard
    cols = width // n_sec
    events = emb.shape[1]
    nbrs = gap.shape[0]
    core = lax.rem(shard, 2)
    sibling = shard + 1 - 2 * core
    picks_src, picks = (picks_src0, picks_src1), (picks0, picks1)
    part_src, part = (part_src0, part_src1), (part0, part1)
    back_src, back = (back_src0, back_src1), (back0, back1)
    hot = (hot0, hot1)

    def drain(ref, sem):
        pltpu.make_async_copy(ref, ref, sem).wait()

    def to_all(step):
        secs = [wrap(sec + j, n_sec) for j in range(n_sec)]

        def go(j, carry):
            d = wrap(shard + j, n_shard)
            for s in secs:
                step(s, d)
            return carry

        for s in secs[1:]:
            step(s, shard)
        lax.fori_loop(1, n_shard, go, 0)

    loads = []
    for i, (far, near_ref) in enumerate(((memory_hbm, memory), (w_in_hbm, w_in), (w_hid_hbm, w_hid))):
        load = pltpu.make_async_copy(far, near_ref, load_sems.at[i])
        load.start()
        loads.append(load)
    barrier = pltpu.get_barrier_semaphore()
    to_all(
        lambda s, d: pl.semaphore_signal(barrier, inc=1, device_id=(s, d), device_id_type=MESH)
    )

    for s in range(n_sec):
        x_src[s] = messages[:, s * cols : (s + 1) * cols].astype(F32)
    x_all[sec] = x_src[sec]
    marks[...] = jnp.full(marks.shape, -1, jnp.int32)
    for b in range(BATCHES):
        marks[b : b + 1, 0:n_shard] = jnp.where(sec < counts[b], slot_rows[b], -1)
    all_marks[me] = marks[...]
    weights = ((w_qkv, f_qkv), (w_out, f_out), (w_time, f_time))
    own = []
    for i, (w, full) in enumerate(weights):
        k = w.shape[0]
        copy = pltpu.make_async_copy(
            w, full.at[pl.ds(pl.multiple_of(sec * k, k), k)], own_sems.at[i]
        )
        copy.start()
        own.append(copy)

    pl.semaphore_wait(barrier, devices - 1)

    def send_marks(s, d):
        pltpu.make_async_remote_copy(
            marks, all_marks.at[me], send_sems.at[0], recv_sems.at[0], (s, d), MESH
        ).start()

    to_all(send_marks)
    for j in range(1, n_sec):
        s = wrap(sec + j, n_sec)
        pltpu.make_async_remote_copy(
            x_src.at[s], x_all.at[sec], send_sems.at[1], recv_sems.at[1], (s, shard), MESH
        ).start()
    for i, (w, full) in enumerate(weights):
        k = w.shape[0]
        half = k // 2
        here = pl.multiple_of(core * half, half)
        there = pl.multiple_of(sec * k + core * half, half)
        for j in range(1, n_sec):
            s = wrap(sec + j, n_sec)
            pltpu.make_async_remote_copy(
                w.at[pl.ds(here, half)],
                full.at[pl.ds(there, half)],
                bulk_send.at[i],
                bulk_recv.at[i],
                (s, shard),
                MESH,
            ).start()

    freq_column = jnp.transpose(jnp.broadcast_to(freq[...], (8, freq.shape[1])))[:, :1]
    phase_column = jnp.transpose(jnp.broadcast_to(phase[...], (8, phase.shape[1])))[:, :1]

    def time_codes(b):
        for n in range(nbrs):
            x = freq_column * gap[n, b : b + 1, :] + phase_column
            te[b, :, n * events : (n + 1) * events] = cosine(x).astype(BF16)

    time_codes(0)

    drain(all_marks.at[pl.ds(0, devices - 1)], recv_sems.at[0])
    lane = lax.broadcasted_iota(jnp.int32, (devices, 128), 1)
    node = lax.broadcasted_iota(jnp.int32, (devices, nodes), 1)
    for b in range(BATCHES):
        row = jnp.sum(jnp.where(lane == shard, all_marks[:, b, :], 0), axis=1, keepdims=True)
        hot[b][...] = jnp.where(row == node, 1.0, 0.0).astype(BF16)
    columns = pl.ds(pl.multiple_of(sec * cols, cols), cols)
    loads[0].wait()
    mine = memory[:, columns]

    def send_picks(b, rows):
        for s in range(n_sec):
            block = rows[s * n_shard : (s + 1) * n_shard]
            picks_src[b][:, s, :] = block
        picks[b][shard] = picks_src[b][shard]

        def go(j, carry):
            d = wrap(shard + j, n_shard)
            pltpu.make_async_remote_copy(
                picks_src[b].at[d],
                picks[b].at[shard],
                send_sems.at[2 + b],
                recv_sems.at[2 + b],
                (sec, d),
                MESH,
            ).start()
            return carry

        lax.fori_loop(1, n_shard, go, 0)

    send_picks(0, dot(hot0[...], mine))
    before = dot(hot1[...], mine)
    match = dot(hot1[...], hot0[...], (1, 1))
    fresh_rows = jnp.sum(match, axis=1, keepdims=True)
    match = match.astype(BF16)

    loads[1].wait()
    drain(x_all.at[pl.ds(0, n_sec - 1)], recv_sems.at[1])
    for b in range(BATCHES):
        rows = jnp.concatenate(
            [x_all[s, b * pool : (b + 1) * pool, :] for s in range(n_sec)], axis=0
        )
        gates_x[b] = dot(rows.astype(BF16), w_in[...])
    time_codes(1)
    loads[2].wait()

    def send_parts(b):
        drain(picks[b].at[pl.ds(0, n_shard - 1)], recv_sems.at[2 + b])
        h = jnp.concatenate([picks[b][:, s, :] for s in range(n_sec)], axis=0)
        gh = dot(h.astype(BF16), w_hid[...])
        gx = gates_x[b]
        low = gx[:, : 2 * width] + gh[:, : 2 * width]
        every = jnp.concatenate([low, gx[:, 2 * width :], gh[:, 2 * width :], h, h], axis=1)
        half = every.shape[1] // 2
        for s in range(n_sec):
            block = every[s * pool : (s + 1) * pool]
            part_src[b][s] = jnp.concatenate([block[:, :half], block[:, half:]], axis=0).astype(BF16)
        part[b][sec] = part_src[b][sec]
        for j in range(1, n_sec):
            s = wrap(sec + j, n_sec)
            pltpu.make_async_remote_copy(
                part_src[b].at[s],
                part[b].at[sec],
                send_sems.at[4 + b],
                recv_sems.at[4 + b],
                (s, shard),
                MESH,
            ).start()

    def gru(b):
        drain(part[b].at[pl.ds(0, n_sec - 1)], recv_sems.at[4 + b])
        pieces = [part[b][s].astype(F32) for s in range(n_sec)]
        total = functools.reduce(lambda a, c: a + c, pieces)
        gates = jnp.concatenate([total[:pool], total[pool:]], axis=1)
        h = jnp.concatenate([p[pool:, -cols:] for p in pieces], axis=1)
        both = bias[0:1, :] + bias[1:2, :]
        r = jax.nn.sigmoid(gates[:, :width] + both[:, :width])
        z = jax.nn.sigmoid(gates[:, width : 2 * width] + both[:, width : 2 * width])
        gx_n = gates[:, 2 * width : 3 * width] + bias[0:1, 2 * width :]
        gh_n = gates[:, 3 * width : 4 * width] + bias[1:2, 2 * width :]
        n = jnp.tanh(gx_n + r * gh_n)
        updated = ((1.0 - z) * n + z * h).astype(BF16)
        wide = updated.astype(F32)
        for k in range(n_sec):
            back_src[b][:, k, :] = wide[:, k * cols : (k + 1) * cols]
        back[b][me] = back_src[b][shard]

        def send(s, d):
            pltpu.make_async_remote_copy(
                back_src[b].at[d],
                back[b].at[me],
                send_sems.at[6 + b],
                recv_sems.at[6 + b],
                (s, d),
                MESH,
            ).start()

        to_all(send)
        return updated

    def forward():
        for copy in own:
            copy.wait()
        for i, (w, full) in enumerate(weights):
            k = w.shape[0]
            half = k // 2
            drain(full.at[pl.ds(0, (n_sec - 1) * half)], bulk_recv.at[i])
            for j in range(1, n_sec):
                s = wrap(sec + j, n_sec)
                place = full.at[pl.ds(pl.multiple_of(s * k + core * half, half), half)]
                pltpu.make_async_remote_copy(
                    place, place, fwd_send.at[i], fwd_recv.at[i], (sec, sibling), MESH
                ).start()

    def gathered():
        for i, (w, full) in enumerate(weights):
            drain(full.at[pl.ds(0, (n_sec - 1) * (w.shape[0] // 2))], fwd_recv.at[i])

    def attend(b, updated):
        qkv = dot(updated, f_qkv[...])
        query = qkv[:, :width]
        keys = qkv[:, width : 2 * width].astype(BF16)
        values = qkv[:, 2 * width :].astype(BF16)
        slot = lax.broadcasted_iota(jnp.int32, (pool, events), 0)
        source = (slot == src[b : b + 1, :]).astype(F32)
        hot_source = source.astype(BF16)
        near = [(slot == nbr[n, b : b + 1, :]).astype(F32) for n in range(nbrs)]
        codes = [te[b, :, n * events : (n + 1) * events] for n in range(nbrs)]
        scale = HD ** -0.5
        mixed, turned, tables = [], [], []
        for head in range(HEADS):
            low = head * HD
            q = jnp.concatenate(split(query[:, low : low + HD] * scale), axis=0)
            proj = f_time[:, low : low + HD]
            pairs = dot(keys[:, low : low + HD], q, (1, 1))
            p_high, p_low = split(pairs[:, :pool] + pairs[:, pool:])
            tables.append(dot(p_high, hot_source) + dot(p_low, hot_source))
            both = dot(q, proj, (1, 1))
            turned.append(both[:pool] + both[pool:])
        turned = jnp.concatenate(turned, axis=0)
        timed = dot(jnp.concatenate(split(turned), axis=0), te[b])
        timed = timed[: HEADS * pool] + timed[HEADS * pool :]
        for head in range(HEADS):
            low = head * HD
            scores = []
            for n in range(nbrs):
                here = timed[head * pool : (head + 1) * pool, n * events : (n + 1) * events]
                scores.append(
                    jnp.sum(here * source + tables[head] * near[n], axis=0, keepdims=True)
                )
            top = functools.reduce(jnp.maximum, scores)
            powers = [jnp.exp(x - top) for x in scores]
            inverse = 1.0 / functools.reduce(lambda a, c: a + c, powers)
            shares = [x * inverse for x in powers]
            by_code = shares[0] * codes[0].astype(F32)
            by_slot = shares[0] * near[0]
            for n in range(1, nbrs):
                by_code = by_code + shares[n] * codes[n].astype(F32)
                by_slot = by_slot + shares[n] * near[n]
            low_v = width + low
            mixed.append(
                dot(by_code.astype(BF16), f_time[:, low_v : low_v + HD], (0, 0))
                + dot(by_slot.astype(BF16), values[:, low : low + HD], (0, 0))
            )
        joined = jnp.concatenate(mixed, axis=1).astype(BF16)
        emb[b] = dot(joined, f_out[...]).astype(BF16)

    def returned(b, k):
        return back[b][:, k, :].astype(BF16)

    send_parts(0)
    updated0 = gru(0)

    drain(back0.at[pl.ds(0, devices - 1)], recv_sems.at[6])
    changed = returned(0, 0)
    for k in range(1, n_sec):
        changed = jnp.where(sec == k, returned(0, k), changed)
    send_picks(1, jnp.where(fresh_rows > 0.5, dot(match, changed), before))

    def write(b, old):
        rows = [returned(b, k) for k in range(n_sec)]
        rows = jnp.concatenate(rows + [jnp.ones((devices, cols), BF16)], axis=1)
        tile = 256
        for t in range(0, nodes, tile):
            new = dot(hot[b][:, t : t + tile], rows, (0, 0))
            hit = new[:, width:] > 0.5
            for k in range(n_sec):
                spot = slice(k * cols, (k + 1) * cols)
                kept = old[t : t + tile, spot]
                memory_out[t : t + tile, spot] = jnp.where(
                    hit, new[:, spot], kept.astype(F32)
                ).astype(BF16)

    write(0, memory)
    forward()
    send_parts(1)
    gathered()
    attend(0, updated0)
    updated1 = gru(1)
    attend(1, updated1)
    drain(back1.at[pl.ds(0, devices - 1)], recv_sems.at[7])
    write(1, memory_out)

    drain(all_marks.at[pl.ds(0, devices - 1)], send_sems.at[0])
    drain(x_all.at[pl.ds(0, n_sec - 1)], send_sems.at[1])
    for b in range(BATCHES):
        drain(picks[b].at[pl.ds(0, n_shard - 1)], send_sems.at[2 + b])
        drain(part[b].at[pl.ds(0, n_sec - 1)], send_sems.at[4 + b])
        drain(back[b].at[pl.ds(0, devices - 1)], send_sems.at[6 + b])
    for i, (w, full) in enumerate(weights):
        rows = pl.ds(0, (n_sec - 1) * (w.shape[0] // 2))
        drain(full.at[rows], bulk_send.at[i])
        drain(full.at[rows], fwd_send.at[i])


def body(
    n_sec,
    n_shard,
    memory,
    messages,
    slot_rows,
    counts,
    src_slot,
    nbr_slots,
    time_gap,
    time_freq,
    time_phase,
    gru_input,
    gru_hidden,
    gru_bias,
    attn_qkv,
    attn_out,
    time_proj,
):
    width = memory.shape[1]
    nodes = memory.shape[0]
    pool = n_shard
    cols = width // n_sec
    events = src_slot.shape[1]
    nbrs = nbr_slots.shape[2]
    tw = time_freq.shape[0]
    devices = n_sec * n_shard
    far = pl.BlockSpec(memory_space=pl.ANY)
    near = pl.BlockSpec(memory_space=pltpu.VMEM)
    wide = (4 * width + 2 * cols) // 2
    out = pl.pallas_call(
        functools.partial(kernel, n_sec, n_shard),
        out_shape=(
            jax.ShapeDtypeStruct((nodes, width), BF16),
            jax.ShapeDtypeStruct((BATCHES, events, width), BF16),
        ),
        in_specs=[far] + [near] * 8 + [far] * 2 + [near] + [far] * 3,
        out_specs=(pl.BlockSpec(memory_space=pltpu.VMEM),) * 2,
        scratch_shapes=[
            pltpu.VMEM((devices, 8, 128), jnp.int32),
            pltpu.VMEM((n_sec, BATCHES * pool, cols), F32),
            pltpu.VMEM((n_sec, BATCHES * pool, cols), F32),
            pltpu.VMEM((n_shard, 8, cols), F32),
            pltpu.VMEM((n_shard, 8, cols), F32),
            pltpu.VMEM((n_shard, 8, cols), F32),
            pltpu.VMEM((n_shard, 8, cols), F32),
            pltpu.VMEM((n_sec, 2 * pool, wide), BF16),
            pltpu.VMEM((n_sec, 2 * pool, wide), BF16),
            pltpu.VMEM((n_sec, 2 * pool, wide), BF16),
            pltpu.VMEM((n_sec, 2 * pool, wide), BF16),
            pltpu.VMEM((n_shard, 8, cols), F32),
            pltpu.VMEM((n_shard, 8, cols), F32),
            pltpu.VMEM((devices, 8, cols), F32),
            pltpu.VMEM((devices, 8, cols), F32),
            pltpu.VMEM((devices, nodes), BF16),
            pltpu.VMEM((devices, nodes), BF16),
            pltpu.VMEM((BATCHES, n_sec * pool, 3 * width), F32),
            pltpu.VMEM((BATCHES, tw, nbrs * events), BF16),
            pltpu.VMEM((width, 3 * width), BF16),
            pltpu.VMEM((width, width), BF16),
            pltpu.VMEM((tw, 2 * width), BF16),
            pltpu.SemaphoreType.DMA((8,)),
            pltpu.SemaphoreType.DMA((8,)),
            pltpu.SemaphoreType.DMA((3,)),
            pltpu.SemaphoreType.DMA((3,)),
            pltpu.SemaphoreType.DMA((3,)),
            pltpu.SemaphoreType.DMA((3,)),
            pltpu.SemaphoreType.DMA((3,)),
            pltpu.VMEM((nodes, width), BF16),
            pltpu.VMEM(gru_input.shape, BF16),
            pltpu.VMEM(gru_hidden.shape, BF16),
            pltpu.SemaphoreType.DMA((3,)),
            pltpu.VMEM((8, 128), jnp.int32),
        ],
        compiler_params=pltpu.CompilerParams(
            collective_id=0, has_side_effects=True, vmem_limit_bytes=56 * 1024 * 1024
        ),
    )(
        memory,
        messages.reshape(BATCHES * pool, width),
        slot_rows.reshape(BATCHES, 1, n_shard),
        counts,
        src_slot,
        nbr_slots.transpose(2, 0, 1),
        time_gap.transpose(2, 0, 1),
        time_freq.reshape(1, tw),
        time_phase.reshape(1, tw),
        gru_input,
        gru_hidden,
        gru_bias,
        attn_qkv,
        attn_out,
        time_proj,
    )
    return out


def solution(mesh):
    in_specs = (
        P("shard", None),
        P(None, "shard", None, "section", None),
        P(None, "shard", None, "section"),
        P(None, "shard", None),
        P(None, ("section", "shard")),
        P(None, ("section", "shard"), None),
        P(None, ("section", "shard"), None),
        P(),
        P(),
        P("section", None),
        P("section", None),
        P(),
        P("section", None),
        P("section", None),
        P("section", None),
    )
    out_specs = (P("shard", None), P(None, ("section", "shard"), None))
    program = functools.partial(body, mesh.shape["section"], mesh.shape["shard"])
    return jax.shard_map(program, mesh=mesh, in_specs=in_specs, out_specs=out_specs, check_vma=False)
```
